32 devices in a mesh: tile: 2 (over y), blk: 16 (over z, x, core).
Axes of the slice: x: 2, y: 2, z: 4, core: 2. Of those that a mesh axis runs over, the one named last changes fastest.
Arguments:
- source_points: float32 [8, 32768], P(None, ('tile', 'blk')), parts along dimension 1, may hold values from -6 to 6
- target_points: float32 [8, 8192], P(None, ('tile', 'blk')), parts along dimension 1, may hold values from -6 to 6
- target_potential: float32 [8192], P(('tile', 'blk')), parts along dimension 0, may hold values from -3 to 3
- target_mass: float32 [8192], P(('tile', 'blk')), parts along dimension 0, may hold values from 0.1 to 10
Outputs:
- potential_update: float32 [32768], P(('tile', 'blk')), parts along dimension 0
- dual_value: float32 [2], P('tile'), parts along dimension 0
The draws below stay inside these ranges and needn't reach their ends.
There are 2 independent parts, one for each index of `tile`. The reference program is written for one: setup_inputs(seed, part) draws one part's arguments, and reference() takes and returns one part's arrays. A program takes and returns all parts, laid end to end along the dimension named above; each array names one. Nothing has to cross between parts.
All inputs are finite; a program needn't handle non-finite values.
Results may differ from the reference program's by a relative error of at most 0.000059.
Values sent between devices are 32-bit elements; how exact they have to be, the bound alone decides.
A program may use at most 64 MiB of HBM per device.

```python
import math
import jax
import jax.numpy as jnp
from jax import lax

FEAT = 8
NSRC = 16384
NTGT = 4096


def shard_levels(rng, dims, cuts, least, largest):
    level, own = 1.0, jax.random.fold_in(rng, 6)
    for dim, blocks in cuts:
        draws = jnp.exp(jax.random.uniform(jax.random.fold_in(own, dim), (blocks,), jnp.float32, least / len(cuts), largest / len(cuts)))
        level = level * jnp.repeat(draws, dims[dim] // blocks).reshape([-1 if axis == dim else 1 for axis in range(len(dims))])
    return level


def scatter_about(own_key, shape, spread, most, cuts=(), kind=jnp.bfloat16):
    gain = shard_levels(own_key, shape, cuts, -0.22, 0.18) if cuts else 1.0
    result = jax.random.normal(own_key, shape, jnp.float32) * spread * gain
    return jnp.minimum(jnp.maximum(result, -most), most).astype(kind)


def setup_inputs(seed: int = 0, part: int = 0) -> dict:
    streams_of = jax.random.split(jax.random.key(seed), 5)
    part_splits = jax.random.split(jax.random.fold_in(streams_of[4], part), 5)
    return {
        "source_points": scatter_about(part_splits[0], (FEAT, NSRC), 1.0, 6.0, ((1, 16),), jnp.float32),
        "target_points": scatter_about(part_splits[1], (FEAT, NTGT), 1.0, 6.0, ((1, 16),), jnp.float32),
        "target_potential": scatter_about(part_splits[2], (NTGT,), 0.5, 3.0, ((0, 16),), jnp.float32),
        "target_mass": jnp.clip(jnp.exp(math.log(10.0) - 4.6051702 * jax.random.uniform(part_splits[3], (NTGT,), jnp.float32) ** shard_levels(part_splits[3], (NTGT,), ((0, 16),), -0.2, 0.2)), 0.1, 10.0),
    }


blur_scale = 0.1


def block_scores(sources, source_sq, portion):
    points = portion[:-2]
    potential = portion[-2]
    log_mass = portion[-1]
    target_sq = jnp.sum(points * points, axis=0)
    inner = lax.dot_general(sources, points, (((0,), (0,)), ((), ())), precision=lax.Precision.HIGHEST, preferred_element_type=jnp.float32)
    distance = source_sq[:, None] + target_sq[None, :] - 2.0 * inner
    return log_mass[None, :] + (potential[None, :] - distance) / blur_scale


def reference(source_points, target_points, target_potential, target_mass):
    log_mass = jnp.log(target_mass)
    stacked = jnp.concatenate([target_points, target_potential[None, :], log_mass[None, :]], axis=0)
    width = math.gcd(NSRC, 512)
    blocks = source_points.reshape(FEAT, NSRC // width, width).transpose(1, 0, 2)

    def one_block(sources):
        source_sq = jnp.sum(sources * sources, axis=0)
        scores = block_scores(sources, source_sq, stacked)
        highest = jnp.max(scores, axis=1)
        return highest + jnp.log(jnp.sum(jnp.exp(scores - highest[:, None]), axis=1))

    lse_values = lax.map(one_block, blocks).reshape(NSRC)
    mass_total = jnp.sum(target_mass)
    potential_update = -blur_scale * (lse_values - jnp.log(mass_total))
    dual_value = jnp.mean(potential_update) + jnp.sum(target_mass * target_potential) / mass_total
    return potential_update, dual_value.reshape(1)
```

```python
import functools
import math

import jax
import jax.numpy as jnp
from jax import lax
from jax.experimental import pallas as pl
from jax.experimental.pallas import tpu as pltpu
from jax.sharding import PartitionSpec as P

blur_scale = 0.1
LOG2E = 1.0 / math.log(2.0)
LN2 = math.log(2.0)
LANES = 128
WIDE = 256


def split3(value):
    high = value.astype(jnp.bfloat16)
    rest = value - high.astype(jnp.float32)
    middle = rest.astype(jnp.bfloat16)
    low = (rest - middle.astype(jnp.float32)).astype(jnp.bfloat16)
    f32 = jnp.float32
    return high.astype(f32), middle.astype(f32), low.astype(f32)


def kernel(
    n, x_ref, y_ref, pot_ref, mass_ref, out_ref, dual_ref,
    gathered, own_sum, sums, rhs_ref, high_ref, total_ref,
    send_sem, recv_sem, sum_send, sum_recv,
):
    me = lax.axis_index("blk")
    feats, rows = x_ref.shape
    cols = y_ref.shape[1]
    f32 = jnp.float32

    barrier = pltpu.get_barrier_semaphore()

    def greet(k, carry):
        peer = lax.rem(me + k, n)
        pl.semaphore_signal(barrier, inc=1, device_id={"blk": peer}, device_id_type=pl.DeviceIdType.MESH)
        return carry

    lax.fori_loop(1, n, greet, 0)

    y = y_ref[...]
    mass = mass_ref[...]
    pot = pot_ref[...]
    bias_rows = cols // LANES
    y_sq = jnp.sum(y * y, axis=0, keepdims=True)
    own_mass = jnp.sum(mass)
    own_weighted = jnp.sum(mass * pot)
    gathered[0, :, pl.ds(0, cols)] = y
    scaled = (jnp.log(mass) + pot * (1.0 / blur_scale)) * LOG2E
    for r in range(bias_rows):
        part = slice(r * LANES, (r + 1) * LANES)
        gathered[0, pl.ds(r, 1), pl.ds(cols, LANES)] = (
            scaled[r : r + 1, :] - y_sq[:, part] * (LOG2E / blur_scale)
        )
    gathered[0, pl.ds(6, 1), pl.ds(cols, LANES)] = jnp.full((1, LANES), own_mass, f32)
    gathered[0, pl.ds(7, 1), pl.ds(cols, LANES)] = jnp.full((1, LANES), own_weighted, f32)

    def message(k):
        peer = lax.rem(me + k, n)
        return pltpu.make_async_remote_copy(
            src_ref=gathered.at[0],
            dst_ref=gathered.at[k],
            send_sem=send_sem.at[k],
            recv_sem=recv_sem.at[k],
            device_id={"blk": peer},
            device_id_type=pl.DeviceIdType.MESH,
        )

    pl.semaphore_wait(barrier, n - 1)

    def send(k, carry):
        message(k).start()
        return carry

    lax.fori_loop(1, n, send, 0)

    x = x_ref[...]
    xh, xm, xl = split3(x * (2.0 * LOG2E / blur_scale))
    row = lax.broadcasted_iota(jnp.int32, (feats, rows), 0)
    ones = jnp.where(row < 3, 1.0, 0.0).astype(f32)
    zeros = jnp.zeros((feats, rows), f32)
    rhs_ref[...] = jnp.concatenate([xh, xm, xh, xl, xh, xm, ones, zeros], axis=0).astype(jnp.bfloat16)

    def absorb(k, first):
        block = gathered[k]
        points = block[:, :cols]
        yh, ym, yl = split3(points)
        bias = jnp.concatenate(
            [block[r : r + 1, cols:] for r in range(bias_rows)], axis=1
        )
        bh, bm, bl = split3(bias)
        tail = jnp.zeros((feats * 2 - 3, cols), f32)
        lhs = jnp.concatenate([yh, yh, ym, yh, yl, ym, bh, bm, bl, tail], axis=0).astype(jnp.bfloat16)
        for c in range(rows // WIDE):
            part = pl.ds(c * WIDE, WIDE)
            t = lax.dot_general(
                lhs, rhs_ref[:, part], (((0,), (0,)), ((), ())), preferred_element_type=f32
            ).reshape(cols // 8, 8, WIDE)
            top = jnp.max(t, axis=0)
            if first:
                high_ref[:, part] = top
                total_ref[:, part] = jnp.sum(jnp.exp2(t - top[None]), axis=0)
            else:
                old = high_ref[:, part]
                high = jnp.maximum(old, top)
                high_ref[:, part] = high
                total_ref[:, part] = total_ref[:, part] * jnp.exp2(old - high) + jnp.sum(
                    jnp.exp2(t - high[None]), axis=0
                )

    absorb(0, True)

    def step(k, carry):
        message(k).wait_recv()
        absorb(k, False)
        return carry

    lax.fori_loop(1, n, step, 0)

    high = high_ref[...]
    top = jnp.max(high, axis=0, keepdims=True)
    total = jnp.sum(total_ref[...] * jnp.exp2(high - top), axis=0, keepdims=True)
    lse = top * LN2 + jnp.log(total)
    raw = jnp.sum(x * x, axis=0, keepdims=True) - blur_scale * lse
    own_sum[...] = jnp.full((1, LANES), jnp.sum(raw), f32)
    sums[0] = own_sum[...]

    def sum_message(k):
        peer = lax.rem(me + k, n)
        return pltpu.make_async_remote_copy(
            src_ref=own_sum,
            dst_ref=sums.at[k],
            send_sem=sum_send.at[k],
            recv_sem=sum_recv.at[k],
            device_id={"blk": peer},
            device_id_type=pl.DeviceIdType.MESH,
        )

    def send_sum(k, carry):
        sum_message(k).start()
        return carry

    lax.fori_loop(1, n, send_sum, 0)

    side = gathered[:, :, cols:]
    mass_total = jnp.sum(side[:, 6, :], axis=0, keepdims=True)
    weighted = jnp.sum(side[:, 7, :], axis=0, keepdims=True)
    shift = blur_scale * jnp.log(mass_total)
    for r in range(rows // LANES):
        out_ref[pl.ds(r, 1), :] = raw[:, r * LANES : (r + 1) * LANES] + shift

    def finish(k, carry):
        message(k).wait_send()
        sum_message(k).wait()
        return carry

    lax.fori_loop(1, n, finish, 0)
    sum_raw = jnp.sum(sums[:, 0, :], axis=0, keepdims=True)
    dual_ref[...] = sum_raw * (1.0 / (n * rows)) + shift + weighted / mass_total


def local(n, source_points, target_points, target_potential, target_mass):
    feats, rows = source_points.shape
    cols = target_points.shape[1]
    f32 = jnp.float32
    vmem = pl.BlockSpec(memory_space=pltpu.VMEM)
    update, dual = pl.pallas_call(
        functools.partial(kernel, n),
        out_shape=(
            jax.ShapeDtypeStruct((rows // LANES, LANES), f32),
            jax.ShapeDtypeStruct((1, LANES), f32),
        ),
        in_specs=[vmem] * 4,
        out_specs=(vmem, vmem),
        scratch_shapes=[
            pltpu.VMEM((n, feats, cols + LANES), f32),
            pltpu.VMEM((1, LANES), f32),
            pltpu.VMEM((n, 1, LANES), f32),
            pltpu.VMEM((8 * feats, rows), jnp.bfloat16),
            pltpu.VMEM((8, rows), f32),
            pltpu.VMEM((8, rows), f32),
            pltpu.SemaphoreType.DMA((n,)),
            pltpu.SemaphoreType.DMA((n,)),
            pltpu.SemaphoreType.DMA((n,)),
            pltpu.SemaphoreType.DMA((n,)),
        ],
        compiler_params=pltpu.CompilerParams(
            collective_id=0, has_side_effects=True, vmem_limit_bytes=32 * 1024 * 1024
        ),
    )(
        source_points,
        target_points,
        target_potential.reshape(cols // LANES, LANES),
        target_mass.reshape(cols // LANES, LANES),
    )
    return update.reshape(rows), dual[0, :1]


def solution(mesh):
    in_specs = (
        P(None, ("tile", "blk")),
        P(None, ("tile", "blk")),
        P(("tile", "blk")),
        P(("tile", "blk")),
    )
    out_specs = (P(("tile", "blk")), P("tile"))
    body = functools.partial(local, mesh.shape["blk"])
    return jax.shard_map(body, mesh=mesh, in_specs=in_specs, out_specs=out_specs, check_vma=False)
```
